256 devices in a mesh: gx: 32 (over z_hi, y, core), ga: 8 (over x, z_lo).
Axes of the slice: x: 4, y: 4, z: 8 (z_hi: 4, z_lo: 2; z = z_hi * 2 + z_lo), core: 2. Of those that a mesh axis runs over, the one named last changes fastest.
Arguments:
- velocity: float32 [6144, 32768], P('gx', 'ga'), may hold values from -12 to 12, as said below
- left_gram: float32 [25, 5], replicated, may hold values from -2.5 to 2.5
- right_gram: float32 [25, 5], replicated, may hold values from -2.5 to 2.5
Outputs:
- x_slope: float32 [6144, 32768], P('gx', 'ga')
- section_field: float32 [6144, 32768], P('gx', 'ga')
The draws below stay inside these ranges and needn't reach their ends.
Inputs may be any that keep to these rules, and one draw needn't show every extreme that they name: velocity at the grid points.
All inputs are finite; a program needn't handle non-finite values.
Results may differ from the reference program's by a relative error of at most 0.000071.
Values sent between devices are 32-bit elements; how exact they have to be, the bound alone decides.
A program may use at most 64 MiB of HBM per device.

```python
import math
import jax
import jax.numpy as jnp
from jax import lax

CONT = 25
DG = 5
NX = 6144
LINES = 32768


def draw_velocity(key, part):
    position = jnp.arange(NX, dtype=jnp.float32)[:, None] / NX
    line_pos = jnp.arange(LINES, dtype=jnp.float32)[None, :] / LINES
    noise = jnp.clip(jax.random.normal(key, (NX, LINES), jnp.float32), -5.0, 5.0)
    amplitude = 0.6 * (1.0 + position) * (1.0 + line_pos)
    return amplitude * noise


def normal_values(stream_key, extent, scale, most, kind=jnp.bfloat16):
    entries = scale * jax.random.normal(stream_key, extent, jnp.float32)
    return jnp.clip(entries, min=-most, max=most).astype(kind)


def setup_inputs(seed: int = 0) -> dict:
    key_list = jax.random.split(jax.random.key(seed), 4)
    return {
        "velocity": draw_velocity(jax.random.fold_in(key_list[3], 71), 0),
        "left_gram": normal_values(key_list[1], (CONT, DG), DG ** -0.5, 2.5, jnp.float32),
        "right_gram": normal_values(key_list[2], (CONT, DG), DG ** -0.5, 2.5, jnp.float32),
    }


courant = 0.5
epsilon = 1e-06

def line_slope(extended):
    period = extended.shape[0]
    spectrum = jnp.fft.rfft(extended, axis=0)
    wavenumber = jnp.arange(spectrum.shape[0], dtype=jnp.float32) * (2.0 * jnp.pi / period)
    slope_all = jnp.fft.irfft(spectrum * (1j * wavenumber)[:, None], n=period, axis=0)
    return slope_all[:NX]

def reference(velocity, left_gram, right_gram):
    line_total = velocity.shape[1]
    block_size = math.gcd(line_total, 512)
    num_blocks = line_total // block_size
    hp = lax.Precision.HIGHEST

    def one_block(which):
        window = lax.dynamic_slice_in_dim(velocity, which * block_size, block_size, 1)
        extension = jnp.dot(left_gram, window[:DG], precision=hp, preferred_element_type=jnp.float32)
        extension = extension + jnp.dot(right_gram, window[NX - DG:], precision=hp, preferred_element_type=jnp.float32)
        extended = jnp.concatenate([window, extension], axis=0)
        return line_slope(extended)
    pieces = lax.map(one_block, jnp.arange(num_blocks, dtype=jnp.int32))
    x_slope = jnp.transpose(pieces, (1, 0, 2)).reshape(NX, line_total)
    mean_square = jnp.mean(velocity * velocity)
    advect_rate = courant / jnp.sqrt(mean_square + epsilon)
    section_field = velocity - advect_rate * velocity * x_slope
    return (x_slope, section_field)
```

```python
import functools
import math

import jax
import jax.numpy as jnp
import ml_dtypes
import numpy as np
from jax import lax
from jax.experimental import pallas as pl
from jax.experimental.pallas import tpu as pltpu
from jax.sharding import PartitionSpec as P

MESH = pl.DeviceIdType.MESH
CONT = 25
DG = 5
NX = 6144
PERIOD = NX + CONT
ROWS = 192
PAIR = 2 * ROWS
LANES = 128
GX = 32
GA = 8
TALL = 768

courant = 0.5
epsilon = 1e-06


def derivative_table():
    shift = np.arange(2 * NX)[:, None] - np.arange(LANES)[None, :] - NX
    shift = shift % PERIOD
    shift = np.where(shift > PERIOD // 2, shift - PERIOD, shift)
    sign = np.where(shift % 2 == 0, 1.0, -1.0)
    angle = np.where(shift == 0, 1.0, shift * (np.pi / PERIOD))
    table = np.where(shift == 0, 0.0, (np.pi / PERIOD) * sign / np.sin(angle))
    high = table.astype(np.float32).astype(ml_dtypes.bfloat16)
    low = (table - high.astype(np.float64)).astype(np.float32).astype(ml_dtypes.bfloat16)
    return high, low


CHIPS = [(0, 0), (0, 1), (0, 3), (0, 2)]
CHIPS += [(dz, dy) for dy in (0, 1, 3, 2) for dz in (1, 3)]
CHIPS += [(2, dy) for dy in (0, 1, 3, 2)]
PEERS = [(dz, dy, dc) for dz, dy in CHIPS for dc in (0, 1)][1:]


def split(values):
    high = values.astype(jnp.bfloat16)
    low = (values - high.astype(jnp.float32)).astype(jnp.bfloat16)
    return jnp.concatenate([high, low], axis=1)


def kernel(
    v_hbm, high_hbm, low_hbm, left_ref, right_ref, slope_ref, rate_ref,
    v, high, low, lines, total, parts, tail, energy, energy_ga, energy_gx,
    local_sem, send_a, recv_a, send_b, recv_b, send_e, recv_e, send_f, recv_f,
):
    me = lax.axis_index("gx")
    group = lax.axis_index("ga")
    z, y, core = me // 8, (me // 2) % 4, me % 2

    def to(o):
        return ((z + o[0]) % 4) * 8 + ((y + o[1]) % 4) * 2 + (core + o[2]) % 2

    def source_chip(o):
        return ((z + 4 - o[0]) % 4) * 4 + (y + 4 - o[1]) % 4

    barrier = pltpu.get_barrier_semaphore()
    for o in PEERS:
        pl.semaphore_signal(barrier, inc=1, device_id={"gx": to(o)}, device_id_type=MESH)
    for k in range(1, GA):
        pl.semaphore_signal(
            barrier, inc=1, device_id={"ga": (group + k) % GA}, device_id_type=MESH
        )
    loads = [
        pltpu.make_async_copy(
            v_hbm.at[:, pl.ds(pl.multiple_of(me * LANES, LANES), LANES)],
            lines.at[pl.ds(pl.multiple_of(me * ROWS, ROWS), ROWS)],
            local_sem.at[0],
        ),
        pltpu.make_async_copy(high_hbm, high, local_sem.at[1]),
        pltpu.make_async_copy(low_hbm, low, local_sem.at[2]),
        pltpu.make_async_copy(v_hbm, v, local_sem.at[3]),
    ]
    for load in loads:
        load.start()
    pl.semaphore_wait(barrier, GX - 1 + GA - 1)

    forward = {}
    for k, o in enumerate(PEERS):
        there = to(o)
        forward[o] = pltpu.make_async_remote_copy(
            src_ref=v_hbm.at[:, pl.ds(pl.multiple_of(there * LANES, LANES), LANES)],
            dst_ref=lines.at[pl.ds(pl.multiple_of(me * ROWS, ROWS), ROWS)],
            send_sem=send_a.at[k],
            recv_sem=recv_a.at[k],
            device_id={"gx": there},
            device_id_type=MESH,
        )
        forward[o].start()

    loads[3].wait()

    def square_rows(i, sums):
        block = v[pl.ds(pl.multiple_of(i * 8, 8), 8), :]
        block = block * block
        for j in range(GX):
            sums = sums + block[:, j * LANES : (j + 1) * LANES]
        return sums

    energy[0] = lax.fori_loop(0, ROWS // 8, square_rows, jnp.zeros((8, LANES), jnp.float32))
    across_ga = []
    for k in range(1, GA):
        across_ga.append(
            pltpu.make_async_remote_copy(
                src_ref=energy.at[0],
                dst_ref=energy_ga.at[k],
                send_sem=send_e.at[k],
                recv_sem=recv_e.at[k],
                device_id={"ga": (group + k) % GA},
                device_id_type=MESH,
            )
        )
        across_ga[-1].start()

    def product(step_base, pieces, row, count, depth):
        tiles = [
            table[pl.ds(pl.multiple_of(row + (NX - 128 * j) - step_base, 128), count), :]
            for table in (high, low)
            for j in range(pieces)
        ]
        if depth:
            tiles += [table[pl.ds(pl.multiple_of(row, 128), count), :] for table in (high, low)]
        both = jnp.dot(
            jnp.concatenate(tiles, axis=1),
            parts[: len(tiles) * 128, :],
            preferred_element_type=jnp.float32,
        )
        return both[:, :LANES] + both[:, LANES:]

    def stage(base):
        pieces = split(lines[pl.ds(pl.multiple_of(base, 128), PAIR), :])
        parts[:PAIR, :] = pieces
        parts[PAIR : 2 * PAIR, :] = pieces

    for load in loads[:3]:
        load.wait()
    for i, chip in enumerate(CHIPS[:-1]):
        for dc in (0, 1):
            if (*chip, dc) in forward:
                forward[(*chip, dc)].wait_recv()
        base = source_chip(chip) * PAIR
        stage(base)

        def rows(r, carry, base=base, first=i == 0):
            row = pl.multiple_of(r * TALL, TALL)
            value = product(base, 3, row, TALL, False)
            here = pl.ds(row, TALL)
            total[here, :] = value if first else total[here, :] + value
            return carry

        lax.fori_loop(0, NX // TALL, rows, 0)
        if i == 4:
            for copy in across_ga:
                copy.wait()
            summed = energy[0]
            for k in range(1, GA):
                summed = summed + energy_ga[k]
            energy[1] = summed
            across_gx = []
            for k, o in enumerate(PEERS):
                across_gx.append(
                    pltpu.make_async_remote_copy(
                        src_ref=energy.at[1],
                        dst_ref=energy_gx.at[k],
                        send_sem=send_f.at[k],
                        recv_sem=recv_f.at[k],
                        device_id={"gx": to(o)},
                        device_id_type=MESH,
                    )
                )
                across_gx[-1].start()

    for dc in (0, 1):
        forward[(*CHIPS[-1], dc)].wait_recv()
    base = source_chip(CHIPS[-1]) * PAIR
    stage(base)
    ends = jnp.zeros((CONT, LANES), jnp.float32)
    for i in range(DG):
        ends = ends + left_ref[:, i : i + 1] * lines[i : i + 1, :]
    for i in range(DG):
        ends = ends + right_ref[:, i : i + 1] * lines[NX - DG + i : NX - DG + i + 1, :]
    tail[...] = jnp.zeros_like(tail)
    tail[:CONT, :] = ends
    pieces = split(tail[...])
    parts[2 * PAIR : 2 * PAIR + 128, :] = pieces
    parts[2 * PAIR + 128 :, :] = pieces

    mine = pl.ds(pl.multiple_of(me * LANES, LANES), LANES)
    back = []
    for chip in CHIPS[1:] + CHIPS[:1]:
        row = pl.multiple_of((to((*chip, 0)) // 2) * PAIR, PAIR)
        total[pl.ds(row, PAIR), :] = total[pl.ds(row, PAIR), :] + product(
            base, 3, row, PAIR, True
        )
        for dc in (0, 1):
            o = (*chip, dc)
            there = to(o)
            source = total.at[pl.ds(pl.multiple_of(there * ROWS, ROWS), ROWS)]
            if o == (0, 0, 0):
                own = pltpu.make_async_copy(source, slope_ref.at[:, mine], local_sem.at[0])
                own.start()
                continue
            k = PEERS.index(o)
            copy = pltpu.make_async_remote_copy(
                src_ref=source,
                dst_ref=slope_ref.at[:, mine],
                send_sem=send_b.at[k],
                recv_sem=recv_b.at[k],
                device_id={"gx": there},
                device_id_type=MESH,
            )
            copy.start()
            back.append(copy)

    for copy in across_gx:
        copy.wait()
    summed = energy[1]
    for k in range(GX - 1):
        summed = summed + energy_gx[k]
    count = NX * LANES * GX * GA
    mean_square = jnp.sum(summed, keepdims=True) / count
    rate = courant / jnp.sqrt(mean_square + epsilon)
    rate_ref[...] = jnp.broadcast_to(rate, (8, LANES))
    for o in PEERS:
        forward[o].wait_send()
    own.wait()
    for copy in back:
        copy.wait()


def per_device(velocity, left_gram, right_gram):
    high, low = derivative_table()
    anywhere = pl.BlockSpec(memory_space=pl.ANY)
    vmem = pl.BlockSpec(memory_space=pltpu.VMEM)
    dma = pltpu.SemaphoreType.DMA
    x_slope, rate = pl.pallas_call(
        kernel,
        out_shape=(
            jax.ShapeDtypeStruct((ROWS, LANES * GX), jnp.float32),
            jax.ShapeDtypeStruct((8, LANES), jnp.float32),
        ),
        in_specs=[anywhere, anywhere, anywhere, vmem, vmem],
        out_specs=(anywhere, vmem),
        scratch_shapes=[
            pltpu.VMEM((ROWS, LANES * GX), jnp.float32),
            pltpu.VMEM((2 * NX, LANES), jnp.bfloat16),
            pltpu.VMEM((2 * NX, LANES), jnp.bfloat16),
            pltpu.VMEM((NX, LANES), jnp.float32),
            pltpu.VMEM((NX, LANES), jnp.float32),
            pltpu.VMEM((2 * PAIR + 256, 2 * LANES), jnp.bfloat16),
            pltpu.VMEM((128, LANES), jnp.float32),
            pltpu.VMEM((2, 8, LANES), jnp.float32),
            pltpu.VMEM((GA, 8, LANES), jnp.float32),
            pltpu.VMEM((GX, 8, LANES), jnp.float32),
            dma((4,)),
            dma((GX - 1,)), dma((GX - 1,)), dma((GX - 1,)), dma((GX - 1,)),
            dma((GA,)), dma((GA,)), dma((GX - 1,)), dma((GX - 1,)),
        ],
        compiler_params=pltpu.CompilerParams(
            collective_id=0, has_side_effects=True, vmem_limit_bytes=48 * 2**20
        ),
        cost_estimate=pl.CostEstimate(
            flops=2 * NX * 2 * NX * 2 * LANES, bytes_accessed=16 * 2**20, transcendentals=0
        ),
        name="exchange_derivative",
    )(velocity, jnp.asarray(high), jnp.asarray(low), left_gram, right_gram)
    advect_rate = rate[0, 0]
    section_field = velocity - advect_rate * velocity * x_slope
    return (x_slope, section_field)


def solution(mesh):
    return jax.shard_map(
        per_device,
        mesh=mesh,
        in_specs=(P("gx", "ga"), P(), P()),
        out_specs=(P("gx", "ga"), P("gx", "ga")),
        check_vma=False,
    )
```

```python
import functools
import math

import jax
import jax.numpy as jnp
import ml_dtypes
import numpy as np
from jax import lax
from jax.experimental import pallas as pl
from jax.experimental.pallas import tpu as pltpu
from jax.sharding import PartitionSpec as P

MESH = pl.DeviceIdType.MESH
CONT = 25
DG = 5
NX = 6144
PERIOD = NX + CONT
ROWS = 192
PAIR = 2 * ROWS
LANES = 128
GX = 32
CHIPS = 16
GA = 8
TALL = 1536

courant = 0.5
epsilon = 1e-06


def derivative_table():
    shift = np.arange(2 * NX)[:, None] - np.arange(LANES)[None, :] - NX
    shift = shift % PERIOD
    shift = np.where(shift > PERIOD // 2, shift - PERIOD, shift)
    sign = np.where(shift % 2 == 0, 1.0, -1.0)
    angle = np.where(shift == 0, 1.0, shift * (np.pi / PERIOD))
    table = np.where(shift == 0, 0.0, (np.pi / PERIOD) * sign / np.sin(angle))
    high = table.astype(np.float32).astype(ml_dtypes.bfloat16)
    low = (table - high.astype(np.float64)).astype(np.float32).astype(ml_dtypes.bfloat16)
    return high, low


AHEAD = 16


def offset(i):
    if isinstance(i, int):
        return (0, i) if i < 4 else ((1, 3, 2)[(i - 4) % 3], (i - 4) // 3)
    near = i < 4
    k = jnp.maximum(i - 4, 0)
    j = k % 3
    return jnp.where(near, 0, 1 + 2 * j - 3 * (j // 2)), jnp.where(near, i, k // 3)


def split(values):
    high = values.astype(jnp.bfloat16)
    low = (values - high.astype(jnp.float32)).astype(jnp.bfloat16)
    return jnp.concatenate([high, low], axis=1)


def kernel(
    v_hbm, high_hbm, low_hbm, left_ref, right_ref, slope_ref, rate_ref,
    v, high, low, lines, total, parts, tail, energy, energy_ga, energy_gx,
    local_sem, send_a, recv_a, send_b, recv_b, send_e, recv_e, send_f, recv_f,
):
    me = lax.axis_index("gx")
    group = lax.axis_index("ga")
    z, y, core = me // 8, (me // 2) % 4, me % 2

    def to(dz, dy, dc):
        return ((z + dz) % 4) * 8 + ((y + dy) % 4) * 2 + (core + dc) % 2

    def source_chip(dz, dy):
        return ((z + 4 - dz) % 4) * 4 + (y + 4 - dy) % 4

    def cores(i):
        return (1,) if isinstance(i, int) and i == 0 else (0, 1)

    barrier = pltpu.get_barrier_semaphore()
    for i in range(CHIPS):
        for dc in cores(i):
            there = to(*offset(i), dc)
            pl.semaphore_signal(barrier, inc=1, device_id={"gx": there}, device_id_type=MESH)
    for k in range(1, GA):
        pl.semaphore_signal(
            barrier, inc=1, device_id={"ga": (group + k) % GA}, device_id_type=MESH
        )
    loads = [
        pltpu.make_async_copy(
            v_hbm.at[:, pl.ds(pl.multiple_of(me * LANES, LANES), LANES)],
            lines.at[pl.ds(pl.multiple_of(me * ROWS, ROWS), ROWS)],
            local_sem.at[0],
        ),
        pltpu.make_async_copy(high_hbm, high, local_sem.at[1]),
        pltpu.make_async_copy(low_hbm, low, local_sem.at[2]),
        pltpu.make_async_copy(v_hbm, v, local_sem.at[3]),
    ]
    for load in loads:
        load.start()
    pl.semaphore_wait(barrier, GX - 1 + GA - 1)

    def forward(i, dc):
        there = to(*offset(i), dc)
        return pltpu.make_async_remote_copy(
            src_ref=v_hbm.at[:, pl.ds(pl.multiple_of(there * LANES, LANES), LANES)],
            dst_ref=lines.at[pl.ds(pl.multiple_of(me * ROWS, ROWS), ROWS)],
            send_sem=send_a.at[2 * i + dc],
            recv_sem=recv_a.at[2 * i + dc],
            device_id={"gx": there},
            device_id_type=MESH,
        )

    def start_forward(i):
        for dc in cores(i):
            forward(i, dc).start()

    for i in range(min(AHEAD, CHIPS)):
        start_forward(i)

    loads[3].wait()

    def square_rows(i, sums):
        block = v[pl.ds(pl.multiple_of(i * 8, 8), 8), :]
        block = block * block
        for j in range(GX):
            sums = sums + block[:, j * LANES : (j + 1) * LANES]
        return sums

    energy[0] = lax.fori_loop(0, ROWS // 8, square_rows, jnp.zeros((8, LANES), jnp.float32))
    across_ga = []
    for k in range(1, GA):
        across_ga.append(
            pltpu.make_async_remote_copy(
                src_ref=energy.at[0],
                dst_ref=energy_ga.at[k],
                send_sem=send_e.at[k],
                recv_sem=recv_e.at[k],
                device_id={"ga": (group + k) % GA},
                device_id_type=MESH,
            )
        )
        across_ga[-1].start()

    def product(step_base, pieces, row, count, depth):
        tiles = [
            table[pl.ds(pl.multiple_of(row + (NX - 128 * j) - step_base, 128), count), :]
            for table in (high, low)
            for j in range(pieces)
        ]
        if depth:
            tiles += [table[pl.ds(pl.multiple_of(row, 128), count), :] for table in (high, low)]
        both = jnp.dot(
            jnp.concatenate(tiles, axis=1),
            parts[: len(tiles) * 128, :],
            preferred_element_type=jnp.float32,
        )
        return both[:, :LANES] + both[:, LANES:]

    def stage(base):
        pieces = split(lines[pl.ds(pl.multiple_of(base, 128), PAIR), :])
        parts[:PAIR, :] = pieces
        parts[PAIR : 2 * PAIR, :] = pieces

    for load in loads[:3]:
        load.wait()

    def work(i, first):
        for dc in cores(i):
            forward(i, dc).wait_recv()
        base = source_chip(*offset(i)) * PAIR
        stage(base)

        def rows(r, carry):
            row = pl.multiple_of(r * TALL, TALL)
            value = product(base, 3, row, TALL, False)
            here = pl.ds(row, TALL)
            total[here, :] = value if first else total[here, :] + value
            return carry

        lax.fori_loop(0, NX // TALL, rows, 0)

    work(0, True)

    def work_and_send(i, carry):
        start_forward(i + AHEAD - 1)
        work(i, False)
        return carry

    def only_work(i, carry):
        work(i, False)
        return carry

    lax.fori_loop(1, max(CHIPS + 1 - AHEAD, 1), work_and_send, 0)
    lax.fori_loop(max(CHIPS + 1 - AHEAD, 1), CHIPS - 1, only_work, 0)

    for dc in (0, 1):
        forward(CHIPS - 1, dc).wait_recv()
    base = source_chip(*offset(CHIPS - 1)) * PAIR
    stage(base)
    ends = jnp.zeros((CONT, LANES), jnp.float32)
    for i in range(DG):
        ends = ends + left_ref[:, i : i + 1] * lines[i : i + 1, :]
    for i in range(DG):
        ends = ends + right_ref[:, i : i + 1] * lines[NX - DG + i : NX - DG + i + 1, :]
    tail[...] = jnp.zeros_like(tail)
    tail[:CONT, :] = ends
    pieces = split(tail[...])
    parts[2 * PAIR : 2 * PAIR + 128, :] = pieces
    parts[2 * PAIR + 128 :, :] = pieces

    for copy in across_ga:
        copy.wait()
    summed = energy[0]
    for k in range(1, GA):
        summed = summed + energy_ga[k]
    energy[1] = summed
    across_gx = []
    for i in range(CHIPS):
        for dc in cores(i):
            across_gx.append(
                pltpu.make_async_remote_copy(
                    src_ref=energy.at[1],
                    dst_ref=energy_gx.at[2 * i + dc],
                    send_sem=send_f.at[2 * i + dc],
                    recv_sem=recv_f.at[2 * i + dc],
                    device_id={"gx": to(*offset(i), dc)},
                    device_id_type=MESH,
                )
            )
            across_gx[-1].start()

    mine = pl.ds(pl.multiple_of(me * LANES, LANES), LANES)

    def backward(i, dc):
        there = to(*offset(i), dc)
        return pltpu.make_async_remote_copy(
            src_ref=total.at[pl.ds(pl.multiple_of(there * ROWS, ROWS), ROWS)],
            dst_ref=slope_ref.at[:, mine],
            send_sem=send_b.at[2 * i + dc],
            recv_sem=recv_b.at[2 * i + dc],
            device_id={"gx": there},
            device_id_type=MESH,
        )

    def finish(i):
        row = pl.multiple_of((to(*offset(i), 0) // 2) * PAIR, PAIR)
        here = pl.ds(row, PAIR)
        total[here, :] = total[here, :] + product(base, 3, row, PAIR, True)
        for dc in cores(i):
            backward(i, dc).start()

    def finish_later(i, carry):
        finish(CHIPS - i)
        return carry

    lax.fori_loop(1, CHIPS, finish_later, 0)
    finish(0)
    own = pltpu.make_async_copy(
        total.at[pl.ds(pl.multiple_of(me * ROWS, ROWS), ROWS)], slope_ref.at[:, mine], local_sem.at[0]
    )
    own.start()

    for copy in across_gx:
        copy.wait()
    summed = energy[1]
    for k in range(1, GX):
        summed = summed + energy_gx[k]
    count = NX * LANES * GX * GA
    mean_square = jnp.sum(summed, keepdims=True) / count
    rate = courant / jnp.sqrt(mean_square + epsilon)
    rate_ref[...] = jnp.broadcast_to(rate, (8, LANES))
    own.wait()

    def wait_all(i, carry):
        for dc in cores(i):
            forward(i, dc).wait_send()
            backward(i, dc).wait()
        return carry

    wait_all(0, 0)
    lax.fori_loop(1, CHIPS, wait_all, 0)


def per_device(velocity, left_gram, right_gram):
    high, low = derivative_table()
    anywhere = pl.BlockSpec(memory_space=pl.ANY)
    vmem = pl.BlockSpec(memory_space=pltpu.VMEM)
    dma = pltpu.SemaphoreType.DMA
    x_slope, rate = pl.pallas_call(
        kernel,
        out_shape=(
            jax.ShapeDtypeStruct((ROWS, LANES * GX), jnp.float32),
            jax.ShapeDtypeStruct((8, LANES), jnp.float32),
        ),
        in_specs=[anywhere, anywhere, anywhere, vmem, vmem],
        out_specs=(anywhere, vmem),
        scratch_shapes=[
            pltpu.VMEM((ROWS, LANES * GX), jnp.float32),
            pltpu.VMEM((2 * NX, LANES), jnp.bfloat16),
            pltpu.VMEM((2 * NX, LANES), jnp.bfloat16),
            pltpu.VMEM((NX, LANES), jnp.float32),
            pltpu.VMEM((NX, LANES), jnp.float32),
            pltpu.VMEM((2 * PAIR + 256, 2 * LANES), jnp.bfloat16),
            pltpu.VMEM((128, LANES), jnp.float32),
            pltpu.VMEM((2, 8, LANES), jnp.float32),
            pltpu.VMEM((GA, 8, LANES), jnp.float32),
            pltpu.VMEM((GX, 8, LANES), jnp.float32),
            dma((4,)),
            dma((GX,)), dma((GX,)), dma((GX,)), dma((GX,)),
            dma((GA,)), dma((GA,)), dma((GX,)), dma((GX,)),
        ],
        compiler_params=pltpu.CompilerParams(
            collective_id=0, has_side_effects=True, vmem_limit_bytes=48 * 2**20
        ),
        cost_estimate=pl.CostEstimate(
            flops=2 * NX * 2 * NX * 2 * LANES, bytes_accessed=16 * 2**20, transcendentals=0
        ),
        name="exchange_derivative",
    )(velocity, jnp.asarray(high), jnp.asarray(low), left_gram, right_gram)
    advect_rate = rate[0, 0]
    section_field = velocity - advect_rate * velocity * x_slope
    return (x_slope, section_field)


def solution(mesh):
    return jax.shard_map(
        per_device,
        mesh=mesh,
        in_specs=(P("gx", "ga"), P(), P()),
        out_specs=(P("gx", "ga"), P("gx", "ga")),
        check_vma=False,
    )
```

```python
import functools
import math

import jax
import jax.numpy as jnp
import ml_dtypes
import numpy as np
from jax import lax
from jax.experimental import pallas as pl
from jax.experimental.pallas import tpu as pltpu
from jax.sharding import PartitionSpec as P

MESH = pl.DeviceIdType.MESH
CONT = 25
DG = 5
NX = 6144
PERIOD = NX + CONT
ROWS = 192
PAIR = 2 * ROWS
LANES = 128
GX = 32
CHIPS = 16
GA = 8
TALL = 1536

courant = 0.5
epsilon = 1e-06


def derivative_table():
    shift = np.arange(2 * NX)[:, None] - np.arange(LANES)[None, :] - NX
    shift = shift % PERIOD
    shift = np.where(shift > PERIOD // 2, shift - PERIOD, shift)
    sign = np.where(shift % 2 == 0, 1.0, -1.0)
    angle = np.where(shift == 0, 1.0, shift * (np.pi / PERIOD))
    table = np.where(shift == 0, 0.0, (np.pi / PERIOD) * sign / np.sin(angle))
    high = table.astype(np.float32).astype(ml_dtypes.bfloat16)
    low = (table - high.astype(np.float64)).astype(np.float32).astype(ml_dtypes.bfloat16)
    return high, low


def offset(i):
    return 2 * (i % 2) + i // 2 % 2, i // 4


def split(values):
    high = values.astype(jnp.bfloat16)
    low = (values - high.astype(jnp.float32)).astype(jnp.bfloat16)
    return jnp.concatenate([high, low], axis=1)


def kernel(
    v_hbm, high_hbm, low_hbm, left_hbm, right_hbm, slope_ref, section_ref,
    v, left, right, high, low, lines, total, parts, tail, energy, energy_ga, energy_gx,
    local_sem, send_a, recv_a, send_b, recv_b, send_e, recv_e, send_f, recv_f,
):
    me = lax.axis_index("gx")
    group = lax.axis_index("ga")
    z, y, core = me // 8, (me // 2) % 4, me % 2

    def to(dz, dy, dc):
        return ((z + dz) % 4) * 8 + ((y + dy) % 4) * 2 + (core + dc) % 2

    def source_chip(dz, dy):
        return ((z + 4 - dz) % 4) * 4 + (y + 4 - dy) % 4

    def cores(i):
        return (1,) if isinstance(i, int) and i == 0 else (0, 1)

    barrier = pltpu.get_barrier_semaphore()
    for i in range(CHIPS):
        for dc in cores(i):
            there = to(*offset(i), dc)
            pl.semaphore_signal(barrier, inc=1, device_id={"gx": there}, device_id_type=MESH)
    for k in range(1, GA):
        pl.semaphore_signal(
            barrier, inc=1, device_id={"ga": (group + k) % GA}, device_id_type=MESH
        )
    loads = [
        pltpu.make_async_copy(
            v_hbm.at[:, pl.ds(pl.multiple_of(me * LANES, LANES), LANES)],
            lines.at[pl.ds(pl.multiple_of(me * ROWS, ROWS), ROWS)],
            local_sem.at[0],
        ),
        pltpu.make_async_copy(high_hbm, high, local_sem.at[1]),
        pltpu.make_async_copy(low_hbm, low, local_sem.at[2]),
        pltpu.make_async_copy(v_hbm, v, local_sem.at[3]),
    ]
    loads += [
        pltpu.make_async_copy(left_hbm, left, local_sem.at[4]),
        pltpu.make_async_copy(right_hbm, right, local_sem.at[5]),
    ]
    for load in loads:
        load.start()
    pl.semaphore_wait(barrier, GX - 1 + GA - 1)

    def forward(i, dc):
        there = to(*offset(i), dc)
        return pltpu.make_async_remote_copy(
            src_ref=v_hbm.at[:, pl.ds(pl.multiple_of(there * LANES, LANES), LANES)],
            dst_ref=lines.at[pl.ds(pl.multiple_of(me * ROWS, ROWS), ROWS)],
            send_sem=send_a.at[2 * i + dc],
            recv_sem=recv_a.at[2 * i + dc],
            device_id={"gx": there},
            device_id_type=MESH,
        )

    def send_to(owner):
        def start_forward(i, carry):
            forward(i, (core + owner) % 2).start()
            return carry

        lax.fori_loop(1, CHIPS, start_forward, 0)

    forward(0, 1).start()
    send_to(0)

    loads[3].wait()

    def square_rows(i, sums):
        block = v[pl.ds(pl.multiple_of(i * 8, 8), 8), :]
        block = block * block
        for j in range(GX):
            sums = sums + block[:, j * LANES : (j + 1) * LANES]
        return sums

    energy[0] = lax.fori_loop(0, ROWS // 8, square_rows, jnp.zeros((8, LANES), jnp.float32))
    across_ga = []
    for k in range(1, GA):
        across_ga.append(
            pltpu.make_async_remote_copy(
                src_ref=energy.at[0],
                dst_ref=energy_ga.at[k],
                send_sem=send_e.at[k],
                recv_sem=recv_e.at[k],
                device_id={"ga": (group + k) % GA},
                device_id_type=MESH,
            )
        )
        across_ga[-1].start()

    send_to(1)

    def product(step_base, pieces, row, count, depth):
        tiles = [
            table[pl.ds(pl.multiple_of(row + (NX - 128 * j) - step_base, 128), count), :]
            for table in (high, low)
            for j in range(pieces)
        ]
        if depth:
            tiles += [table[pl.ds(pl.multiple_of(row, 128), count), :] for table in (high, low)]
        both = jnp.dot(
            jnp.concatenate(tiles, axis=1),
            parts[: len(tiles) * 128, :],
            preferred_element_type=jnp.float32,
        )
        return both[:, :LANES] + both[:, LANES:]

    def stage(base):
        pieces = split(lines[pl.ds(pl.multiple_of(base, 128), PAIR), :])
        parts[:PAIR, :] = pieces
        parts[PAIR : 2 * PAIR, :] = pieces

    for load in loads[:3] + loads[4:]:
        load.wait()

    def work(i, first):
        for dc in cores(i):
            forward(i, dc).wait_recv()
        base = source_chip(*offset(i)) * PAIR
        stage(base)

        def rows(r, carry):
            row = pl.multiple_of(r * TALL, TALL)
            value = product(base, 3, row, TALL, False)
            here = pl.ds(row, TALL)
            total[here, :] = value if first else total[here, :] + value
            return carry

        lax.fori_loop(0, NX // TALL, rows, 0)

    work(0, True)

    def work_later(i, carry):
        work(i, False)
        return carry

    lax.fori_loop(1, CHIPS - 1, work_later, 0)

    for dc in (0, 1):
        forward(CHIPS - 1, dc).wait_recv()
    base = source_chip(*offset(CHIPS - 1)) * PAIR
    stage(base)
    ends = lax.dot_general(
        left[...],
        lines[:DG, :],
        (((0,), (0,)), ((), ())),
        precision=lax.Precision.HIGHEST,
        preferred_element_type=jnp.float32,
    )
    ends = ends + lax.dot_general(
        right[...],
        lines[NX - DG :, :],
        (((0,), (0,)), ((), ())),
        precision=lax.Precision.HIGHEST,
        preferred_element_type=jnp.float32,
    )
    tail[...] = jnp.zeros_like(tail)
    tail[:CONT, :] = ends
    pieces = split(tail[...])
    parts[2 * PAIR : 2 * PAIR + 128, :] = pieces
    parts[2 * PAIR + 128 :, :] = pieces

    for copy in across_ga:
        copy.wait()
    summed = energy[0]
    for k in range(1, GA):
        summed = summed + energy_ga[k]
    energy[1] = summed
    across_gx = []
    for i in range(CHIPS):
        for dc in cores(i):
            across_gx.append(
                pltpu.make_async_remote_copy(
                    src_ref=energy.at[1],
                    dst_ref=energy_gx.at[2 * i + dc],
                    send_sem=send_f.at[2 * i + dc],
                    recv_sem=recv_f.at[2 * i + dc],
                    device_id={"gx": to(*offset(i), dc)},
                    device_id_type=MESH,
                )
            )
            across_gx[-1].start()

    mine = pl.ds(pl.multiple_of(me * LANES, LANES), LANES)

    def backward(i, dc):
        there = to(*offset(i), dc)
        return pltpu.make_async_remote_copy(
            src_ref=total.at[pl.ds(pl.multiple_of(there * ROWS, ROWS), ROWS)],
            dst_ref=slope_ref.at[:, mine],
            send_sem=send_b.at[2 * i + dc],
            recv_sem=recv_b.at[2 * i + dc],
            device_id={"gx": there},
            device_id_type=MESH,
        )

    def finish(i):
        row = pl.multiple_of((to(*offset(i), 0) // 2) * PAIR, PAIR)
        here = pl.ds(row, PAIR)
        total[here, :] = total[here, :] + product(base, 3, row, PAIR, True)
        for dc in cores(i):
            backward(i, dc).start()

    def finish_later(i, carry):
        finish(i)
        return carry

    lax.fori_loop(1, CHIPS, finish_later, 0)
    finish(0)
    own = pltpu.make_async_copy(
        total.at[pl.ds(pl.multiple_of(me * ROWS, ROWS), ROWS)], slope_ref.at[:, mine], local_sem.at[0]
    )
    own.start()

    for copy in across_gx:
        copy.wait()
    summed = energy[1]
    for k in range(1, GX):
        summed = summed + energy_gx[k]
    count = NX * LANES * GX * GA
    mean_square = jnp.sum(summed, keepdims=True) / count
    rate = courant / jnp.sqrt(mean_square + epsilon)

    def section(i, dc):
        there = ((z + 4 - offset(i)[0]) % 4) * 8 + ((y + 4 - offset(i)[1]) % 4) * 2 + (core + dc) % 2
        here = pl.ds(pl.multiple_of(there * LANES, LANES), LANES)
        block = v[:, here]
        section_ref[:, here] = block - rate * block * slope_ref[:, here]

    def receive(i, dc):
        backward(i, dc).wait_recv()
        section(i, dc)

    own.wait()
    section(0, 0)
    for sender in (0, 1):

        def receive_later(i, carry, sender=sender):
            receive(i, (core + sender) % 2)
            return carry

        lax.fori_loop(1, CHIPS, receive_later, 0)
    receive(0, 1)

    def wait_sent(i, carry):
        for dc in cores(i):
            forward(i, dc).wait_send()
            backward(i, dc).wait_send()
        return carry

    wait_sent(0, 0)
    lax.fori_loop(1, CHIPS, wait_sent, 0)


def write_out(slope_vmem, section_vmem, slope_hbm, section_hbm, sem):
    copies = [
        pltpu.make_async_copy(slope_vmem, slope_hbm, sem.at[0]),
        pltpu.make_async_copy(section_vmem, section_hbm, sem.at[1]),
    ]
    for copy in copies:
        copy.start()
    for copy in copies:
        copy.wait()


def per_device(velocity, left_gram, right_gram):
    high, low = derivative_table()
    anywhere = pl.BlockSpec(memory_space=pl.ANY)
    vmem = pl.BlockSpec(memory_space=pltpu.VMEM)
    dma = pltpu.SemaphoreType.DMA
    block = jax.ShapeDtypeStruct((ROWS, LANES * GX), jnp.float32)
    results = pl.pallas_call(
        kernel,
        out_shape=(pltpu.VMEM(block.shape, block.dtype),) * 2,
        in_specs=[pl.BlockSpec(memory_space=pltpu.HBM)] * 5,
        out_specs=(vmem, vmem),
        scratch_shapes=[
            pltpu.VMEM((ROWS, LANES * GX), jnp.float32),
            pltpu.VMEM((DG, CONT), jnp.float32),
            pltpu.VMEM((DG, CONT), jnp.float32),
            pltpu.VMEM((2 * NX, LANES), jnp.bfloat16),
            pltpu.VMEM((2 * NX, LANES), jnp.bfloat16),
            pltpu.VMEM((NX, LANES), jnp.float32),
            pltpu.VMEM((NX, LANES), jnp.float32),
            pltpu.VMEM((2 * PAIR + 256, 2 * LANES), jnp.bfloat16),
            pltpu.VMEM((128, LANES), jnp.float32),
            pltpu.VMEM((2, 8, LANES), jnp.float32),
            pltpu.VMEM((GA, 8, LANES), jnp.float32),
            pltpu.VMEM((GX, 8, LANES), jnp.float32),
            dma((6,)),
            dma((GX,)), dma((GX,)), dma((GX,)), dma((GX,)),
            dma((GA,)), dma((GA,)), dma((GX,)), dma((GX,)),
        ],
        compiler_params=pltpu.CompilerParams(
            collective_id=0, has_side_effects=True, vmem_limit_bytes=48 * 2**20
        ),
        cost_estimate=pl.CostEstimate(
            flops=2 * NX * 2 * NX * 2 * LANES, bytes_accessed=16 * 2**20, transcendentals=0
        ),
        name="exchange_derivative",
    )(velocity, jnp.asarray(high), jnp.asarray(low), left_gram.T, right_gram.T)
    return pl.pallas_call(
        write_out,
        out_shape=(block, block),
        in_specs=[anywhere] * 2,
        out_specs=(anywhere, anywhere),
        scratch_shapes=[dma((2,))],
        compiler_params=pltpu.CompilerParams(vmem_limit_bytes=2**20),
        name="write_out",
    )(*results)


def solution(mesh):
    return jax.shard_map(
        per_device,
        mesh=mesh,
        in_specs=(P("gx", "ga"), P(), P()),
        out_specs=(P("gx", "ga"), P("gx", "ga")),
        check_vma=False,
    )
```

```python
import functools
import math

import jax
import jax.numpy as jnp
import ml_dtypes
import numpy as np
from jax import lax
from jax.experimental import pallas as pl
from jax.experimental.pallas import tpu as pltpu
from jax.sharding import PartitionSpec as P

MESH = pl.DeviceIdType.MESH
CONT = 25
DG = 5
NX = 6144
PERIOD = NX + CONT
ROWS = 192
PAIR = 2 * ROWS
LANES = 128
GX = 32
CHIPS = 16
MIDWAY = 10
GA = 8
TALL = 1536

courant = 0.5
epsilon = 1e-06


def derivative_table():
    shift = np.arange(2 * NX)[:, None] - np.arange(LANES)[None, :] - NX
    shift = shift % PERIOD
    shift = np.where(shift > PERIOD // 2, shift - PERIOD, shift)
    sign = np.where(shift % 2 == 0, 1.0, -1.0)
    angle = np.where(shift == 0, 1.0, shift * (np.pi / PERIOD))
    table = np.where(shift == 0, 0.0, (np.pi / PERIOD) * sign / np.sin(angle))
    high = table.astype(np.float32).astype(ml_dtypes.bfloat16)
    low = (table - high.astype(np.float64)).astype(np.float32).astype(ml_dtypes.bfloat16)
    return high, low


def offset(i):
    return 2 * (i % 2) + i // 2 % 2, i // 4


def split(values):
    high = values.astype(jnp.bfloat16)
    low = (values - high.astype(jnp.float32)).astype(jnp.bfloat16)
    return jnp.concatenate([high, low], axis=1)


def kernel(
    v_hbm, high_hbm, low_hbm, left_hbm, right_hbm, slope_ref, section_ref,
    v, left, right, high, low, lines, total, parts, tail, energy, energy_ga, energy_gx,
    local_sem, send_a, recv_a, send_b, recv_b, send_e, recv_e, send_f, recv_f,
):
    me = lax.axis_index("gx")
    group = lax.axis_index("ga")
    z, y, core = me // 8, (me // 2) % 4, me % 2

    def to(dz, dy, dc):
        return ((z + dz) % 4) * 8 + ((y + dy) % 4) * 2 + (core + dc) % 2

    def source_chip(dz, dy):
        return ((z + 4 - dz) % 4) * 4 + (y + 4 - dy) % 4

    def cores(i):
        return (1,) if isinstance(i, int) and i == 0 else (0, 1)

    barrier = pltpu.get_barrier_semaphore()
    for i in range(CHIPS):
        for dc in cores(i):
            there = to(*offset(i), dc)
            pl.semaphore_signal(barrier, inc=1, device_id={"gx": there}, device_id_type=MESH)
    for k in range(1, GA):
        pl.semaphore_signal(
            barrier, inc=1, device_id={"ga": (group + k) % GA}, device_id_type=MESH
        )
    loads = [
        pltpu.make_async_copy(
            v_hbm.at[:, pl.ds(pl.multiple_of(me * LANES, LANES), LANES)],
            lines.at[pl.ds(pl.multiple_of(me * ROWS, ROWS), ROWS)],
            local_sem.at[0],
        ),
        pltpu.make_async_copy(high_hbm, high, local_sem.at[1]),
        pltpu.make_async_copy(low_hbm, low, local_sem.at[2]),
        pltpu.make_async_copy(v_hbm, v, local_sem.at[3]),
    ]
    loads += [
        pltpu.make_async_copy(left_hbm, left, local_sem.at[4]),
        pltpu.make_async_copy(right_hbm, right, local_sem.at[5]),
    ]
    for load in loads:
        load.start()
    pl.semaphore_wait(barrier, GX - 1 + GA - 1)

    def forward(i, dc):
        there = to(*offset(i), dc)
        return pltpu.make_async_remote_copy(
            src_ref=v_hbm.at[:, pl.ds(pl.multiple_of(there * LANES, LANES), LANES)],
            dst_ref=lines.at[pl.ds(pl.multiple_of(me * ROWS, ROWS), ROWS)],
            send_sem=send_a.at[2 * i + dc],
            recv_sem=recv_a.at[2 * i + dc],
            device_id={"gx": there},
            device_id_type=MESH,
        )

    def send_to(owner):
        def start_forward(i, carry):
            forward(i, (core + owner) % 2).start()
            return carry

        lax.fori_loop(1, CHIPS, start_forward, 0)

    forward(0, 1).start()
    send_to(0)

    loads[3].wait()

    def square_rows(i, sums):
        block = v[pl.ds(pl.multiple_of(i * 8, 8), 8), :]
        block = block * block
        for j in range(GX):
            sums = sums + block[:, j * LANES : (j + 1) * LANES]
        return sums

    energy[0] = lax.fori_loop(0, ROWS // 8, square_rows, jnp.zeros((8, LANES), jnp.float32))
    across_ga = []
    for k in range(1, GA):
        across_ga.append(
            pltpu.make_async_remote_copy(
                src_ref=energy.at[0],
                dst_ref=energy_ga.at[k],
                send_sem=send_e.at[k],
                recv_sem=recv_e.at[k],
                device_id={"ga": (group + k) % GA},
                device_id_type=MESH,
            )
        )
        across_ga[-1].start()

    send_to(1)

    def product(step_base, pieces, row, count, depth):
        tiles = [
            table[pl.ds(pl.multiple_of(row + (NX - 128 * j) - step_base, 128), count), :]
            for table in (high, low)
            for j in range(pieces)
        ]
        if depth:
            tiles += [table[pl.ds(pl.multiple_of(row, 128), count), :] for table in (high, low)]
        both = jnp.dot(
            jnp.concatenate(tiles, axis=1),
            parts[: len(tiles) * 128, :],
            preferred_element_type=jnp.float32,
        )
        return both[:, :LANES] + both[:, LANES:]

    def stage(base):
        pieces = split(lines[pl.ds(pl.multiple_of(base, 128), PAIR), :])
        parts[:PAIR, :] = pieces
        parts[PAIR : 2 * PAIR, :] = pieces

    for load in loads[:3] + loads[4:]:
        load.wait()

    def work(i, first):
        for dc in cores(i):
            forward(i, dc).wait_recv()
        base = source_chip(*offset(i)) * PAIR
        stage(base)

        def rows(r, carry):
            row = pl.multiple_of(r * TALL, TALL)
            value = product(base, 3, row, TALL, False)
            here = pl.ds(row, TALL)
            total[here, :] = value if first else total[here, :] + value
            return carry

        lax.fori_loop(0, NX // TALL, rows, 0)

    work(0, True)

    def work_later(i, carry):
        work(i, False)
        return carry

    lax.fori_loop(1, MIDWAY, work_later, 0)

    def exchange(value, slot, offsets):
        energy[slot] = value
        copies = []
        for k, (dz, dy, dc) in offsets:
            copies.append(
                pltpu.make_async_remote_copy(
                    src_ref=energy.at[slot],
                    dst_ref=energy_gx.at[k],
                    send_sem=send_f.at[k],
                    recv_sem=recv_f.at[k],
                    device_id={"gx": to(dz, dy, dc)},
                    device_id_type=MESH,
                )
            )
            copies[-1].start()
        return copies

    for copy in across_ga:
        copy.wait()
    summed = energy[0]
    for k in range(1, GA):
        summed = summed + energy_ga[k]
    across_y = exchange(summed, 1, [(k, (0, k // 2, k % 2)) for k in range(1, 8)])

    lax.fori_loop(MIDWAY, CHIPS - 1, work_later, 0)

    for dc in (0, 1):
        forward(CHIPS - 1, dc).wait_recv()
    base = source_chip(*offset(CHIPS - 1)) * PAIR
    stage(base)
    ends = lax.dot_general(
        left[...],
        lines[:DG, :],
        (((0,), (0,)), ((), ())),
        precision=lax.Precision.HIGHEST,
        preferred_element_type=jnp.float32,
    )
    ends = ends + lax.dot_general(
        right[...],
        lines[NX - DG :, :],
        (((0,), (0,)), ((), ())),
        precision=lax.Precision.HIGHEST,
        preferred_element_type=jnp.float32,
    )
    tail[...] = jnp.zeros_like(tail)
    tail[:CONT, :] = ends
    pieces = split(tail[...])
    parts[2 * PAIR : 2 * PAIR + 128, :] = pieces
    parts[2 * PAIR + 128 :, :] = pieces

    mine = pl.ds(pl.multiple_of(me * LANES, LANES), LANES)

    def backward(i, dc):
        there = to(*offset(i), dc)
        return pltpu.make_async_remote_copy(
            src_ref=total.at[pl.ds(pl.multiple_of(there * ROWS, ROWS), ROWS)],
            dst_ref=slope_ref.at[:, mine],
            send_sem=send_b.at[2 * i + dc],
            recv_sem=recv_b.at[2 * i + dc],
            device_id={"gx": there},
            device_id_type=MESH,
        )

    def finish(i):
        row = pl.multiple_of((to(*offset(i), 0) // 2) * PAIR, PAIR)
        here = pl.ds(row, PAIR)
        total[here, :] = total[here, :] + product(base, 3, row, PAIR, True)
        for dc in cores(i):
            backward(i, dc).start()

    def finish_later(i, carry):
        finish(i)
        return carry

    lax.fori_loop(1, CHIPS // 2, finish_later, 0)
    for copy in across_y:
        copy.wait()
    summed = energy[1]
    for k in range(1, 8):
        summed = summed + energy_gx[k]
    across_z = exchange(summed, 2, [(8 + k, (k, 0, 0)) for k in range(1, 4)])
    lax.fori_loop(CHIPS // 2, CHIPS, finish_later, 0)
    finish(0)
    own = pltpu.make_async_copy(
        total.at[pl.ds(pl.multiple_of(me * ROWS, ROWS), ROWS)], slope_ref.at[:, mine], local_sem.at[0]
    )
    own.start()

    for copy in across_z:
        copy.wait()
    summed = energy[2]
    for k in range(9, 12):
        summed = summed + energy_gx[k]
    count = NX * LANES * GX * GA
    mean_square = jnp.sum(summed, keepdims=True) / count
    rate = courant / jnp.sqrt(mean_square + epsilon)

    def section(i, dc):
        there = ((z + 4 - offset(i)[0]) % 4) * 8 + ((y + 4 - offset(i)[1]) % 4) * 2 + (core + dc) % 2
        here = pl.ds(pl.multiple_of(there * LANES, LANES), LANES)
        block = v[:, here]
        section_ref[:, here] = block - rate * block * slope_ref[:, here]

    def receive(i, dc):
        backward(i, dc).wait_recv()
        section(i, dc)

    own.wait()
    section(0, 0)
    for sender in (0, 1):

        def receive_later(i, carry, sender=sender):
            receive(i, (core + sender) % 2)
            return carry

        lax.fori_loop(1, CHIPS, receive_later, 0)
    receive(0, 1)

    def wait_sent(i, carry):
        for dc in cores(i):
            forward(i, dc).wait_send()
            backward(i, dc).wait_send()
        return carry

    wait_sent(0, 0)
    lax.fori_loop(1, CHIPS, wait_sent, 0)


def write_out(slope_vmem, section_vmem, slope_hbm, section_hbm, sem):
    copies = [
        pltpu.make_async_copy(slope_vmem, slope_hbm, sem.at[0]),
        pltpu.make_async_copy(section_vmem, section_hbm, sem.at[1]),
    ]
    for copy in copies:
        copy.start()
    for copy in copies:
        copy.wait()


def per_device(velocity, left_gram, right_gram):
    high, low = derivative_table()
    anywhere = pl.BlockSpec(memory_space=pl.ANY)
    vmem = pl.BlockSpec(memory_space=pltpu.VMEM)
    dma = pltpu.SemaphoreType.DMA
    block = jax.ShapeDtypeStruct((ROWS, LANES * GX), jnp.float32)
    results = pl.pallas_call(
        kernel,
        out_shape=(pltpu.VMEM(block.shape, block.dtype),) * 2,
        in_specs=[pl.BlockSpec(memory_space=pltpu.HBM)] * 5,
        out_specs=(vmem, vmem),
        scratch_shapes=[
            pltpu.VMEM((ROWS, LANES * GX), jnp.float32),
            pltpu.VMEM((DG, CONT), jnp.float32),
            pltpu.VMEM((DG, CONT), jnp.float32),
            pltpu.VMEM((2 * NX, LANES), jnp.bfloat16),
            pltpu.VMEM((2 * NX, LANES), jnp.bfloat16),
            pltpu.VMEM((NX, LANES), jnp.float32),
            pltpu.VMEM((NX, LANES), jnp.float32),
            pltpu.VMEM((2 * PAIR + 256, 2 * LANES), jnp.bfloat16),
            pltpu.VMEM((128, LANES), jnp.float32),
            pltpu.VMEM((3, 8, LANES), jnp.float32),
            pltpu.VMEM((GA, 8, LANES), jnp.float32),
            pltpu.VMEM((12, 8, LANES), jnp.float32),
            dma((6,)),
            dma((GX,)), dma((GX,)), dma((GX,)), dma((GX,)),
            dma((GA,)), dma((GA,)), dma((12,)), dma((12,)),
        ],
        compiler_params=pltpu.CompilerParams(
            collective_id=0, has_side_effects=True, vmem_limit_bytes=48 * 2**20
        ),
        cost_estimate=pl.CostEstimate(
            flops=2 * NX * 2 * NX * 2 * LANES, bytes_accessed=16 * 2**20, transcendentals=0
        ),
        name="exchange_derivative",
    )(velocity, jnp.asarray(high), jnp.asarray(low), left_gram.T, right_gram.T)
    return pl.pallas_call(
        write_out,
        out_shape=(block, block),
        in_specs=[anywhere] * 2,
        out_specs=(anywhere, anywhere),
        scratch_shapes=[dma((2,))],
        compiler_params=pltpu.CompilerParams(vmem_limit_bytes=2**20),
        name="write_out",
    )(*results)


def solution(mesh):
    return jax.shard_map(
        per_device,
        mesh=mesh,
        in_specs=(P("gx", "ga"), P(), P()),
        out_specs=(P("gx", "ga"), P("gx", "ga")),
        check_vma=False,
    )
```

```python
import functools
import math

import jax
import jax.numpy as jnp
import ml_dtypes
import numpy as np
from jax import lax
from jax.experimental import pallas as pl
from jax.experimental.pallas import tpu as pltpu
from jax.sharding import PartitionSpec as P

MESH = pl.DeviceIdType.MESH
CONT = 25
DG = 5
NX = 6144
PERIOD = NX + CONT
ROWS = 192
PAIR = 2 * ROWS
LANES = 128
GX = 32
CHIPS = 16
MIDWAY = 10
PARTS = 4
GA = 8
TALL = 1536

courant = 0.5
epsilon = 1e-06


def derivative_table():
    shift = np.arange(2 * NX)[:, None] - np.arange(LANES)[None, :] - NX
    shift = shift % PERIOD
    shift = np.where(shift > PERIOD // 2, shift - PERIOD, shift)
    sign = np.where(shift % 2 == 0, 1.0, -1.0)
    angle = np.where(shift == 0, 1.0, shift * (np.pi / PERIOD))
    table = np.where(shift == 0, 0.0, (np.pi / PERIOD) * sign / np.sin(angle))
    high = table.astype(np.float32).astype(ml_dtypes.bfloat16)
    low = (table - high.astype(np.float64)).astype(np.float32).astype(ml_dtypes.bfloat16)
    return high, low


def offset(i):
    return 2 * (i % 2) + i // 2 % 2, i // 4


def split(values):
    high = values.astype(jnp.bfloat16)
    low = (values - high.astype(jnp.float32)).astype(jnp.bfloat16)
    return jnp.concatenate([high, low], axis=1)


def kernel(
    v_hbm, high_hbm, low_hbm, left_hbm, right_hbm, slope_ref, section_ref,
    v, left, right, high, low, lines, total, parts, tail, energy, energy_ga, energy_gx,
    local_sem, send_a, recv_a, send_b, recv_b, send_e, recv_e, send_f, recv_f,
):
    me = lax.axis_index("gx")
    group = lax.axis_index("ga")
    z, y, core = me // 8, (me // 2) % 4, me % 2

    def to(dz, dy, dc):
        return ((z + dz) % 4) * 8 + ((y + dy) % 4) * 2 + (core + dc) % 2

    def source_chip(dz, dy):
        return ((z + 4 - dz) % 4) * 4 + (y + 4 - dy) % 4

    def cores(i):
        return (1,) if isinstance(i, int) and i == 0 else (0, 1)

    barrier = pltpu.get_barrier_semaphore()
    for i in range(CHIPS):
        for dc in cores(i):
            there = to(*offset(i), dc)
            pl.semaphore_signal(barrier, inc=1, device_id={"gx": there}, device_id_type=MESH)
    for k in range(1, GA):
        pl.semaphore_signal(
            barrier, inc=1, device_id={"ga": (group + k) % GA}, device_id_type=MESH
        )
    loads = [
        pltpu.make_async_copy(
            v_hbm.at[:, pl.ds(pl.multiple_of(me * LANES, LANES), LANES)],
            lines.at[pl.ds(pl.multiple_of(me * ROWS, ROWS), ROWS)],
            local_sem.at[0],
        ),
        pltpu.make_async_copy(high_hbm, high, local_sem.at[1]),
        pltpu.make_async_copy(low_hbm, low, local_sem.at[2]),
        pltpu.make_async_copy(v_hbm, v, local_sem.at[3]),
    ]
    loads += [
        pltpu.make_async_copy(left_hbm, left, local_sem.at[4]),
        pltpu.make_async_copy(right_hbm, right, local_sem.at[5]),
    ]
    for load in loads:
        load.start()
    pl.semaphore_wait(barrier, GX - 1 + GA - 1)

    def forward(i, dc):
        there = to(*offset(i), dc)
        return pltpu.make_async_remote_copy(
            src_ref=v_hbm.at[:, pl.ds(pl.multiple_of(there * LANES, LANES), LANES)],
            dst_ref=lines.at[pl.ds(pl.multiple_of(me * ROWS, ROWS), ROWS)],
            send_sem=send_a.at[2 * i + dc],
            recv_sem=recv_a.at[2 * i + dc],
            device_id={"gx": there},
            device_id_type=MESH,
        )

    def send_to(owner):
        def start_forward(i, carry):
            forward(i, (core + owner) % 2).start()
            return carry

        lax.fori_loop(1, CHIPS, start_forward, 0)

    forward(0, 1).start()
    send_to(0)

    loads[3].wait()

    def square_rows(i, sums):
        block = v[pl.ds(pl.multiple_of(i * 8, 8), 8), :]
        block = block * block
        for j in range(GX):
            sums = sums + block[:, j * LANES : (j + 1) * LANES]
        return sums

    energy[0] = lax.fori_loop(0, ROWS // 8, square_rows, jnp.zeros((8, LANES), jnp.float32))
    across_ga = []
    for k in range(1, GA):
        across_ga.append(
            pltpu.make_async_remote_copy(
                src_ref=energy.at[0],
                dst_ref=energy_ga.at[k],
                send_sem=send_e.at[k],
                recv_sem=recv_e.at[k],
                device_id={"ga": (group + k) % GA},
                device_id_type=MESH,
            )
        )
        across_ga[-1].start()

    send_to(1)

    def product(step_base, pieces, row, count, depth):
        tiles = [
            table[pl.ds(pl.multiple_of(row + (NX - 128 * j) - step_base, 128), count), :]
            for table in (high, low)
            for j in range(pieces)
        ]
        if depth:
            tiles += [table[pl.ds(pl.multiple_of(row, 128), count), :] for table in (high, low)]
        both = jnp.dot(
            jnp.concatenate(tiles, axis=1),
            parts[: len(tiles) * 128, :],
            preferred_element_type=jnp.float32,
        )
        return both[:, :LANES] + both[:, LANES:]

    def stage(base):
        pieces = split(lines[pl.ds(pl.multiple_of(base, 128), PAIR), :])
        parts[:PAIR, :] = pieces
        parts[PAIR : 2 * PAIR, :] = pieces

    for load in loads[:3] + loads[4:]:
        load.wait()

    def work(i, first):
        for dc in cores(i):
            forward(i, dc).wait_recv()
        base = source_chip(*offset(i)) * PAIR
        stage(base)

        def rows(r, carry):
            row = pl.multiple_of(r * TALL, TALL)
            value = product(base, 3, row, TALL, False)
            here = pl.ds(row, TALL)
            total[here, :] = value if first else total[here, :] + value
            return carry

        lax.fori_loop(0, NX // TALL, rows, 0)

    work(0, True)

    def work_later(i, carry):
        work(i, False)
        return carry

    lax.fori_loop(1, MIDWAY, work_later, 0)

    def exchange(value, slot, offsets):
        energy[slot] = value
        copies = []
        for k, (dz, dy, dc) in offsets:
            copies.append(
                pltpu.make_async_remote_copy(
                    src_ref=energy.at[slot],
                    dst_ref=energy_gx.at[k],
                    send_sem=send_f.at[k],
                    recv_sem=recv_f.at[k],
                    device_id={"gx": to(dz, dy, dc)},
                    device_id_type=MESH,
                )
            )
            copies[-1].start()
        return copies

    for copy in across_ga:
        copy.wait()
    summed = energy[0]
    for k in range(1, GA):
        summed = summed + energy_ga[k]
    across_y = exchange(summed, 1, [(k, (0, k // 2, k % 2)) for k in range(1, 8)])

    lax.fori_loop(MIDWAY, CHIPS - 1, work_later, 0)

    for dc in (0, 1):
        forward(CHIPS - 1, dc).wait_recv()
    base = source_chip(*offset(CHIPS - 1)) * PAIR
    stage(base)
    ends = lax.dot_general(
        left[...],
        lines[:DG, :],
        (((0,), (0,)), ((), ())),
        precision=lax.Precision.HIGHEST,
        preferred_element_type=jnp.float32,
    )
    ends = ends + lax.dot_general(
        right[...],
        lines[NX - DG :, :],
        (((0,), (0,)), ((), ())),
        precision=lax.Precision.HIGHEST,
        preferred_element_type=jnp.float32,
    )
    tail[...] = jnp.zeros_like(tail)
    tail[:CONT, :] = ends
    pieces = split(tail[...])
    parts[2 * PAIR : 2 * PAIR + 128, :] = pieces
    parts[2 * PAIR + 128 :, :] = pieces

    mine = pl.ds(pl.multiple_of(me * LANES, LANES), LANES)

    def backward(i, dc):
        there = to(*offset(i), dc)
        return pltpu.make_async_remote_copy(
            src_ref=total.at[pl.ds(pl.multiple_of(there * ROWS, ROWS), ROWS)],
            dst_ref=slope_ref.at[:, mine],
            send_sem=send_b.at[2 * i + dc],
            recv_sem=recv_b.at[2 * i + dc],
            device_id={"gx": there},
            device_id_type=MESH,
        )

    def finish(i):
        row = pl.multiple_of((to(*offset(i), 0) // 2) * PAIR, PAIR)
        here = pl.ds(row, PAIR)
        total[here, :] = total[here, :] + product(base, 3, row, PAIR, True)
        for dc in cores(i):
            backward(i, dc).start()

    def finish_later(i, carry):
        finish(i)
        return carry

    lax.fori_loop(1, CHIPS // 2, finish_later, 0)
    for copy in across_y:
        copy.wait()
    summed = energy[1]
    for k in range(1, 8):
        summed = summed + energy_gx[k]
    across_z = exchange(summed, 2, [(8 + k, (k, 0, 0)) for k in range(1, 4)])
    lax.fori_loop(CHIPS // 2, CHIPS, finish_later, 0)
    finish(0)
    own = pltpu.make_async_copy(
        total.at[pl.ds(pl.multiple_of(me * ROWS, ROWS), ROWS)], slope_ref.at[:, mine], local_sem.at[0]
    )
    own.start()

    for copy in across_z:
        copy.wait()
    summed = energy[2]
    for k in range(9, 12):
        summed = summed + energy_gx[k]
    count = NX * LANES * GX * GA
    mean_square = jnp.sum(summed, keepdims=True) / count
    rate = courant / jnp.sqrt(mean_square + epsilon)

    def section(i, dc):
        there = ((z + 4 - offset(i)[0]) % 4) * 8 + ((y + 4 - offset(i)[1]) % 4) * 2 + (core + dc) % 2
        here = pl.ds(pl.multiple_of(there * LANES, LANES), LANES)
        block = v[:, here]
        section_ref[:, here] = block - rate * block * slope_ref[:, here]

    def receive(i, dc):
        forward(i, dc).wait_send()
        backward(i, dc).wait()
        section(i, dc)

    own.wait()
    section(0, 0)
    for sender in (0, 1):

        def receive_later(i, carry, sender=sender):
            receive(i, (core + sender) % 2)
            return carry

        lax.fori_loop(1, CHIPS, receive_later, 0)
    receive(0, 1)


def write_out(slope_vmem, section_vmem, slope_hbm, section_hbm, sem):
    part = ROWS // PARTS
    copies = [
        pltpu.make_async_copy(
            source.at[pl.ds(k * part, part)], target.at[pl.ds(k * part, part)], sem.at[PARTS * n + k]
        )
        for k in range(PARTS)
        for n, (source, target) in enumerate(
            ((slope_vmem, slope_hbm), (section_vmem, section_hbm))
        )
    ]
    for copy in copies:
        copy.start()
    for copy in copies:
        copy.wait()


def per_device(velocity, left_gram, right_gram):
    high, low = derivative_table()
    anywhere = pl.BlockSpec(memory_space=pl.ANY)
    vmem = pl.BlockSpec(memory_space=pltpu.VMEM)
    dma = pltpu.SemaphoreType.DMA
    block = jax.ShapeDtypeStruct((ROWS, LANES * GX), jnp.float32)
    results = pl.pallas_call(
        kernel,
        out_shape=(pltpu.VMEM(block.shape, block.dtype),) * 2,
        in_specs=[pl.BlockSpec(memory_space=pltpu.HBM)] * 5,
        out_specs=(vmem, vmem),
        scratch_shapes=[
            pltpu.VMEM((ROWS, LANES * GX), jnp.float32),
            pltpu.VMEM((DG, CONT), jnp.float32),
            pltpu.VMEM((DG, CONT), jnp.float32),
            pltpu.VMEM((2 * NX, LANES), jnp.bfloat16),
            pltpu.VMEM((2 * NX, LANES), jnp.bfloat16),
            pltpu.VMEM((NX, LANES), jnp.float32),
            pltpu.VMEM((NX, LANES), jnp.float32),
            pltpu.VMEM((2 * PAIR + 256, 2 * LANES), jnp.bfloat16),
            pltpu.VMEM((128, LANES), jnp.float32),
            pltpu.VMEM((3, 8, LANES), jnp.float32),
            pltpu.VMEM((GA, 8, LANES), jnp.float32),
            pltpu.VMEM((12, 8, LANES), jnp.float32),
            dma((6,)),
            dma((GX,)), dma((GX,)), dma((GX,)), dma((GX,)),
            dma((GA,)), dma((GA,)), dma((12,)), dma((12,)),
        ],
        compiler_params=pltpu.CompilerParams(
            collective_id=0, has_side_effects=True, vmem_limit_bytes=48 * 2**20
        ),
        cost_estimate=pl.CostEstimate(
            flops=2 * NX * 2 * NX * 2 * LANES, bytes_accessed=16 * 2**20, transcendentals=0
        ),
        name="exchange_derivative",
    )(velocity, jnp.asarray(high), jnp.asarray(low), left_gram.T, right_gram.T)
    return pl.pallas_call(
        write_out,
        out_shape=(block, block),
        in_specs=[anywhere] * 2,
        out_specs=(anywhere, anywhere),
        scratch_shapes=[dma((2 * PARTS,))],
        compiler_params=pltpu.CompilerParams(vmem_limit_bytes=2**20),
        name="write_out",
    )(*results)


def solution(mesh):
    return jax.shard_map(
        per_device,
        mesh=mesh,
        in_specs=(P("gx", "ga"), P(), P()),
        out_specs=(P("gx", "ga"), P("gx", "ga")),
        check_vma=False,
    )
```
